32 devices in a mesh: dp: 8 (over y, x, core), mp: 4 (over z).
Axes of the slice: x: 2, y: 2, z: 4, core: 2. Of those that a mesh axis runs over, the one named last changes fastest.
Arguments:
- image_latents: bfloat16 [16, 48, 3072], P('dp', None, 'mp'), may hold values from -6 to 6
- text_states: bfloat16 [112, 16, 3072], P('dp', None, 'mp'), may hold values from -6 to 6
- modulation: bfloat16 [112, 3, 3072], P('dp', None, 'mp'), may hold values from -2 to 2
- w_qkv: bfloat16 [3072, 3, 2048], P(None, None, 'mp'), may hold values from -0.109375 to 0.109375
- w_out: bfloat16 [2048, 3072], P('mp'), may hold values from -0.125 to 0.125
- q_gain: float32 [128], replicated, may hold values from 1.2 to 3
- k_gain: float32 [128], replicated, may hold values from 1.2 to 3
- branch_count: int32 [16], P('dp'), may hold values from 1 to 7, as said below
- branch_sign: int32 [112], P('dp'), may hold values from 0 to 1
- guide_weight: int32 [112], P('dp'), may hold values from 1 to 8
Outputs:
- prediction: bfloat16 [16, 48, 3072], P('dp', None, 'mp')
The draws below stay inside these ranges and needn't reach their ends.
Inputs may be any that keep to these rules, and one draw needn't show every extreme that they name: `branch_count`: image i and image i + 8 have counts summing to 8, so the counts of all images sum to 64.
All inputs are finite; a program needn't handle non-finite values.
Results may differ from the reference program's by a relative error of at most 0.015.
Values may be sent and summed in bfloat16 or wider, within the bound.
A program may use at most 64 MiB of HBM per device.

```python
import math
import jax
import jax.numpy as jnp
from jax import lax

D = 3072
HEADS = 16
HD = 128
IMG_TOK = 48
TXT_TOK = 16
MAXB = 7
IMG_DEV = 2
IMAGES = 16
L = 64
N_MP = 4


def draw_branch_count(key, part):
    count_key = jax.random.fold_in(key, 11)
    half_count = IMAGES // 2
    first_counts = jax.random.randint(count_key, (half_count,), 1, MAXB + 1)
    first_counts = jnp.where(jnp.arange(half_count) < IMG_DEV, MAXB, first_counts)
    return jnp.concatenate([first_counts, MAXB + 1 - first_counts]).astype(jnp.int32)


def draw_modulation(key, part):
    slot_rows = IMAGES * MAXB
    base_key = jax.random.fold_in(key, 23)
    shift_key = jax.random.fold_in(base_key, 1)
    scale_key = jax.random.fold_in(base_key, 2)
    gate_key = jax.random.fold_in(base_key, 3)
    sign_key = jax.random.fold_in(base_key, 4)
    shift_rows = 0.25 * jax.random.truncated_normal(shift_key, -3.0, 3.0, (slot_rows, 1, D), jnp.float32)
    scale_rows = jax.random.uniform(scale_key, (slot_rows, 1, D), jnp.float32, 0.0, 1.5)
    magnitude = jax.random.uniform(gate_key, (slot_rows, 1, D), jnp.float32, 0.75, 2.0)
    sign_rows = jnp.where(jax.random.bernoulli(sign_key, 0.5, (slot_rows, 1, D)), 1.0, -1.0).astype(jnp.float32)
    gate_rows = sign_rows * magnitude
    return jnp.concatenate([shift_rows, scale_rows, gate_rows], axis=1).astype(jnp.bfloat16)


def with_ends(array, stream_key, least, high):
    longest = array.shape.index(max(array.shape))
    spots = []
    for shift in (0, 1):
        where = [jax.random.randint(jax.random.fold_in(stream_key, axis), (), 0, length) for axis, length in enumerate(array.shape)]
        where[longest] = (where[longest] + shift) % array.shape[longest]
        spots.append(tuple(where))
    return array.at[spots[0]].set(least).at[spots[1]].set(high)


def steps_of(stream_key, dims, cuts, low, high):
    loudness, own = 1.0, jax.random.fold_in(stream_key, 6)
    for axis_at, parts in cuts:
        draws = jnp.exp(jax.random.uniform(jax.random.fold_in(own, axis_at), (parts,), jnp.float32, low / len(cuts), high / len(cuts)))
        loudness = loudness * jnp.repeat(draws, dims[axis_at] // parts).reshape([-1 if axis == axis_at else 1 for axis in range(len(dims))])
    return loudness


def normal_values(rng, dims, width, reach, split=(), kind=jnp.bfloat16):
    entries = jax.random.normal(rng, dims, jnp.float32) * width
    if len(split) > 0:
        entries = steps_of(rng, dims, split, -0.22, 0.18) * entries
    return jnp.clip(entries, min=-reach, max=reach).astype(kind)


def setup_inputs(seed: int = 0) -> dict:
    splits = jax.random.split(jax.random.key(seed), 11)
    return {
        "image_latents": normal_values(splits[0], (IMAGES, IMG_TOK, D), 1.0, 6.0, ((0, 8), (2, 4))),
        "text_states": normal_values(splits[1], (IMAGES * MAXB, TXT_TOK, D), 1.0, 6.0, ((0, 8), (2, 4))),
        "modulation": draw_modulation(jax.random.fold_in(splits[10], 71), 0),
        "w_qkv": normal_values(splits[3], (D, 3, HEADS * HD), D ** -0.5, 0.109375, ((2, 4),)),
        "w_out": normal_values(splits[4], (HEADS * HD, D), (HEADS * HD) ** -0.5, 0.125, ((0, 4),)),
        "q_gain": jnp.clip(jnp.exp(jax.random.uniform(splits[5], (HD,), jnp.float32, math.log(1.2), math.log(3.0))), 1.2, 3.0),
        "k_gain": jnp.clip(jnp.exp(jax.random.uniform(splits[6], (HD,), jnp.float32, math.log(1.2), math.log(3.0))), 1.2, 3.0),
        "branch_count": draw_branch_count(jax.random.fold_in(splits[10], 71), 0),
        "branch_sign": with_ends(jax.random.randint(splits[8], (IMAGES * MAXB,), 0, 2), jax.random.fold_in(splits[8], 1), 0, 1).astype(jnp.int32),
        "guide_weight": with_ends(jax.random.randint(splits[9], (IMAGES * MAXB,), 1, 9), jax.random.fold_in(splits[9], 1), 1, 8).astype(jnp.int32),
    }


epsilon = 1e-06

def rms_norm(values, gain):
    return values * lax.rsqrt(lax.optimization_barrier(jnp.mean(values * values, axis=-1, keepdims=True)) + epsilon) * gain

def block_row(sequence, modulation_rows, w_qkv, w_out, q_gain, k_gain):
    states = sequence.astype(jnp.float32)
    row_mean = lax.optimization_barrier(jnp.mean(states, axis=-1, keepdims=True))
    centered = states - row_mean
    spread = lax.optimization_barrier(jnp.mean(centered * centered, axis=-1, keepdims=True))
    shift_rows = modulation_rows[0].astype(jnp.float32)
    scale_rows = modulation_rows[1].astype(jnp.float32)
    gate_rows = modulation_rows[2].astype(jnp.float32)
    normed = (centered * lax.rsqrt(spread + epsilon) * (1.0 + scale_rows) + shift_rows).astype(jnp.bfloat16)
    projected = jnp.dot(normed, w_qkv.reshape(D, 3 * HEADS * HD), preferred_element_type=jnp.float32)
    projected = projected.reshape(L, 3, HEADS, HD)
    queries = rms_norm(projected[:, 0], q_gain).astype(jnp.bfloat16)
    key_rows = rms_norm(projected[:, 1], k_gain).astype(jnp.bfloat16)
    value_rows = projected[:, 2].astype(jnp.bfloat16)
    scores = jnp.einsum('qhd,khd->hqk', queries.astype(jnp.float32), key_rows.astype(jnp.float32)) * HD ** (-0.5)
    attention_weights = jax.nn.softmax(scores, axis=-1).astype(jnp.bfloat16)
    attended = jnp.einsum('hqk,khd->qhd', attention_weights.astype(jnp.float32), value_rows.astype(jnp.float32)).astype(jnp.bfloat16)
    group_heads = HEADS // N_MP
    image_part = attended[TXT_TOK:].reshape(IMG_TOK, N_MP, group_heads * HD)
    partials = jnp.einsum('tgc,gcd->gtd', image_part.astype(jnp.float32), w_out.reshape(N_MP, group_heads * HD, D).astype(jnp.float32))
    partials = lax.optimization_barrier(partials.astype(jnp.bfloat16)).astype(jnp.float32)
    out_rows = lax.optimization_barrier(jnp.sum(partials, axis=0))
    return (states[TXT_TOK:] + gate_rows * out_rows).astype(jnp.bfloat16)

def reference(image_latents, text_states, modulation, w_qkv, w_out, q_gain, k_gain, branch_count, branch_sign, guide_weight):
    is_live = jnp.arange(MAXB, dtype=jnp.int32)[None, :] < branch_count[:, None]
    weights_live = jnp.where(is_live, guide_weight.reshape(IMAGES, MAXB), 0).astype(jnp.float32)
    weight_total = lax.optimization_barrier(jnp.sum(weights_live, axis=1))
    branch_slots = jnp.nonzero(is_live.reshape(-1), size=4 * IMAGES)[0].astype(jnp.int32)
    branch_image = (branch_slots // MAXB).astype(jnp.int32)
    signs = (2 * branch_sign[branch_slots] - 1).astype(jnp.float32)
    coefficient = signs * guide_weight[branch_slots].astype(jnp.float32) / weight_total[branch_image]

    def branch_output(slot_index):
        image_index = (slot_index // MAXB).astype(jnp.int32)
        sequence = jnp.concatenate([text_states[slot_index], image_latents[image_index]], axis=0)
        return block_row(sequence, modulation[slot_index], w_qkv, w_out, q_gain, k_gain)
    outputs = lax.map(branch_output, branch_slots)
    weighted = coefficient[:, None, None] * outputs.astype(jnp.float32)
    prediction = jax.ops.segment_sum(weighted, branch_image, num_segments=IMAGES)
    return prediction.astype(jnp.bfloat16)
```

```python
import functools

import jax
import jax.numpy as jnp
from jax import lax
from jax.experimental import pallas as pl
from jax.experimental.pallas import tpu as pltpu
from jax.sharding import PartitionSpec as P

EPS = 1e-06
MESH = pl.DeviceIdType.MESH
F32 = jnp.float32
BF16 = jnp.bfloat16


def kernel(
    n, dp, per_image,
    cnt_ref, sgn_ref, gw_ref, img_ref, txt_ref, mod_ref, qg_ref, kg_ref, w_hbm, wo_hbm,
    out_ref,
    w_v, wo_v, ximg, xhat, mod_x, mod_y, mod_g, txt_y, txt_g, coef_x, coef_y,
    nimg, ntxt, q_s, k_s, v_s, att, acc, ysend, yrecv, rsend, rrecv,
    w_sem, zi_s, zi_r, zm_s, zm_r, zt_s, zt_r, yt_s, yt_r, yi_s, yi_r, yo_s, yo_r, zo_s, zo_r,
):
    me = lax.axis_index("mp")
    mine = lax.axis_index("dp")
    partner = lax.rem(mine + dp // 2, dp)
    images, img_len, width = img_ref.shape
    txt_len = txt_ref.shape[1]
    half = (per_image + 1) // 2
    extra = per_image - half
    full = n * width
    heads, hd = q_s.shape[1], q_s.shape[3]
    rows = half * img_len
    items = images * half

    weight_copies = [
        pltpu.make_async_copy(w_hbm.at[t], w_v.at[t], w_sem.at[t]) for t in range(3)
    ] + [
        pltpu.make_async_copy(
            wo_hbm.at[:, pl.ds(o * width, width)], wo_v.at[o], w_sem.at[3 + o]
        )
        for o in range(n)
    ]
    for c in weight_copies:
        c.start()

    def peer(d):
        return lax.rem(me + d, n)

    def source(d):
        return lax.rem(me - d + n, n)

    barrier = pltpu.get_barrier_semaphore()
    for d in range(1, n):
        pl.semaphore_signal(barrier, inc=1, device_id={"mp": peer(d)}, device_id_type=MESH)
    pl.semaphore_signal(barrier, inc=1, device_id={"dp": partner}, device_id_type=MESH)

    slots = images * per_image
    row_at = lax.broadcasted_iota(jnp.int32, coef_x.shape, 0)
    top = jnp.zeros(coef_x.shape, jnp.int32)
    low = jnp.ones(coef_x.shape, jnp.int32)
    for i in range(images):
        total = jnp.int32(0)
        for b in range(per_image):
            s = i * per_image + b
            live = jnp.where(b < cnt_ref[i], gw_ref[s], 0)
            total = total + live
            top = jnp.where(row_at == s, (2 * sgn_ref[s] - 1) * live, top)
        inside = (row_at >= i * per_image) & (row_at < (i + 1) * per_image)
        low = jnp.where(inside, total, low)
    coef_x[...] = top.astype(F32) / low.astype(F32)
    own_mod = [mod_ref[t].astype(F32) for t in range(3)]
    pieces = []
    for t in range(3):
        for i in range(images):
            first = i * per_image + half
            pieces.append(own_mod[t][first : first + extra])
        pieces.append(jnp.zeros((items - images * extra, width), F32))
    pieces.append(jnp.zeros((mod_x.shape[0] - 3 * items, width), F32))
    mod_x[...] = jnp.concatenate(pieces, axis=0).astype(BF16)

    pl.semaphore_wait(barrier, n)

    def to_peer(src, dst, send, recv, d):
        return pltpu.make_async_remote_copy(
            src_ref=src, dst_ref=dst, send_sem=send.at[d - 1], recv_sem=recv.at[d - 1],
            device_id={"mp": peer(d)}, device_id_type=MESH,
        )

    def to_partner(src, dst, send, recv):
        return pltpu.make_async_remote_copy(
            src_ref=src, dst_ref=dst, send_sem=send, recv_sem=recv,
            device_id={"dp": partner}, device_id_type=MESH,
        )

    zi = [to_peer(img_ref, ximg.at[0, me], zi_s, zi_r, d) for d in range(1, n)]
    yt = [to_partner(mod_x, mod_y, yt_s.at[0], yt_r.at[0])]
    for i in range(images):
        yt.append(
            to_partner(
                txt_ref.at[pl.ds(i * per_image + half, extra)], txt_y.at[i],
                yt_s.at[1 + i], yt_r.at[1 + i],
            )
        )
    yt.append(to_partner(coef_x, coef_y, yt_s.at[1 + images], yt_r.at[1 + images]))
    yi = [to_partner(img_ref, ximg.at[1, me], yi_s.at[0], yi_r.at[0])]
    for c in yt:
        c.start()
    for c in zi:
        c.start()
    yi[0].start()
    ximg[0, me] = img_ref[...]

    yt[0].wait_recv()
    got = mod_y[...].astype(F32)
    pieces = []
    for t in range(3):
        for i in range(images):
            for k in range(half):
                s = i * per_image + k
                row = own_mod[t][s : s + 1]
                if k > 0:
                    r = t * items + i * extra + extra - k
                    row = jnp.where(cnt_ref[i] > k, row, got[r : r + 1])
                pieces.append(row)
    pieces.append(jnp.zeros((mod_g.shape[1] - 3 * items, width), F32))
    mod_g[me] = jnp.concatenate(pieces, axis=0).astype(BF16)
    zm = [to_peer(mod_g.at[me], mod_g.at[me], zm_s, zm_r, d) for d in range(1, n)]
    for c in zm:
        c.start()
    zt = []
    for i in range(images):
        yt[1 + i].wait_recv()
        for k in range(half):
            own = txt_ref[i * per_image + k]
            if k > 0:
                own = jnp.where(
                    cnt_ref[i] > k, own.astype(F32), txt_y[i, extra - k].astype(F32)
                ).astype(BF16)
            txt_g[i, me, pl.ds(k * txt_len, txt_len), :] = own
        zt.append(
            [
                to_peer(txt_g.at[i, me], txt_g.at[i, me], zt_s.at[i], zt_r.at[i], d)
                for d in range(1, n)
            ]
        )
        for c in zt[i]:
            c.start()

    for d in range(1, n):
        zi[d - 1].wait_recv()
        o = source(d)
        c = to_partner(ximg.at[0, o], ximg.at[1, o], yi_s.at[d], yi_r.at[d])
        c.start()
        yi.append(c)

    def normalise(parts):
        mean = sum(jnp.sum(p, axis=-1, keepdims=True) for p in parts) * (1.0 / full)
        parts = [p - mean for p in parts]
        var = sum(jnp.sum(p * p, axis=-1, keepdims=True) for p in parts) * (1.0 / full)
        scale = lax.rsqrt(var + EPS)
        return [p * scale for p in parts]

    def image_hat(who):
        for i in range(images):
            parts = normalise([ximg[who, o, i].astype(F32) for o in range(n)])
            for o in range(n):
                xhat[who, i, o] = parts[o]

    image_hat(0)
    for c in zm:
        c.wait_recv()
    for c in yi:
        c.wait_recv()
    image_hat(1)

    for o in range(n):
        mods = mod_g[o].astype(F32)
        for i in range(images):
            for k in range(half):
                p = i * half + k
                who = jnp.where(cnt_ref[i] > k, 0, 1)
                hat = xhat[who, i, o]
                value = hat * (1.0 + mods[items + p : items + p + 1]) + mods[p : p + 1]
                nimg[pl.ds(p * img_len, img_len), pl.ds(o * width, width)] = value.astype(BF16)

    def rms(values, gain):
        mean = jnp.mean(values * values, axis=-1, keepdims=True)
        return values * lax.rsqrt(mean + EPS) * gain

    q_gain, k_gain = qg_ref[...], kg_ref[...]
    for t in range(3):
        weight_copies[t].wait()
        made = jnp.dot(nimg[...], w_v[t], preferred_element_type=F32)
        for h in range(heads):
            part = made[:, h * hd : (h + 1) * hd]
            if t == 0:
                part = rms(part, q_gain)
            if t == 1:
                part = rms(part, k_gain)
            part = part.astype(BF16)
            for i in range(images):
                (q_s, k_s, v_s)[t][i, h, pl.ds(0, rows), :] = part[i * rows : (i + 1) * rows]

    keys = half * (img_len + txt_len)
    q_row = lax.broadcasted_iota(jnp.int32, (rows, keys), 0)
    k_col = lax.broadcasted_iota(jnp.int32, (rows, keys), 1)
    same = jnp.zeros((rows, keys), jnp.bool_)
    for k in range(half):
        in_q = (q_row >= k * img_len) & (q_row < (k + 1) * img_len)
        in_img = (k_col >= k * img_len) & (k_col < (k + 1) * img_len)
        first = rows + k * txt_len
        in_txt = (k_col >= first) & (k_col < first + txt_len)
        same = same | (in_q & (in_img | in_txt))
    bias = jnp.where(same, 0.0, -1e30)

    yt[1 + images].wait_recv()
    for c in weight_copies[3:]:
        c.wait()

    def wide(row):
        return jnp.concatenate([row] * (width // row.shape[1]), axis=1)

    order = list(range(1, n)) + [0]
    yo = []
    for i in range(images):
        for c in zt[i]:
            c.wait_recv()
        parts = normalise([txt_g[i, o].astype(F32) for o in range(n)])
        for o in range(n):
            mods = mod_g[o].astype(F32)
            for k in range(half):
                p = i * half + k
                value = parts[o][k * txt_len : (k + 1) * txt_len]
                value = value * (1.0 + mods[items + p : items + p + 1]) + mods[p : p + 1]
                ntxt[pl.ds(k * txt_len, txt_len), pl.ds(o * width, width)] = value.astype(BF16)
        for t in (1, 2):
            made = jnp.dot(ntxt[...], w_v[t], preferred_element_type=F32)
            for h in range(heads):
                part = made[:, h * hd : (h + 1) * hd]
                if t == 1:
                    part = rms(part, k_gain)
                (k_s if t == 1 else v_s)[i, h, pl.ds(rows, half * txt_len), :] = part.astype(BF16)
        for h in range(heads):
            scores = lax.dot_general(
                q_s[i, h], k_s[i, h], (((1,), (1,)), ((), ())), preferred_element_type=F32
            ) * hd ** (-0.5) + bias
            powers = jnp.exp(scores - jnp.max(scores, axis=-1, keepdims=True))
            probs = powers / jnp.sum(powers, axis=-1, keepdims=True)
            att[:, pl.ds(h * hd, hd)] = jnp.dot(
                probs.astype(BF16), v_s[i, h], preferred_element_type=F32
            ).astype(BF16)
        sent = []
        for d in order:
            o = peer(d)
            part = jnp.dot(att[...], wo_v[o], preferred_element_type=F32).astype(BF16).astype(F32)
            mods = mod_g[o].astype(F32)
            own_sum = jnp.zeros((img_len, width), F32)
            far_sum = jnp.zeros((img_len, width), F32)
            for k in range(half):
                g = 2 * items + i * half + k
                term = part[k * img_len : (k + 1) * img_len] * mods[g : g + 1]
                s = i * per_image + k
                own_sum = own_sum + term * wide(coef_x[s : s + 1, :])
                if k > 0:
                    s = i * per_image + per_image - k
                    far_sum = far_sum + term * wide(coef_y[s : s + 1, :])
            acc[i, o] = own_sum
            ysend[i, o] = far_sum.astype(BF16)
            c = to_partner(ysend.at[i, o], yrecv.at[i, o], yo_s.at[i, d], yo_r.at[i, d])
            c.start()
            sent.append(c)
        yo.append(sent)

    zo = []
    for i in range(images):
        sent = []
        for at, d in enumerate(order):
            o = peer(d)
            yo[i][at].wait_recv()
            value = acc[i, o] + yrecv[i, o].astype(F32)
            if d == 0:
                acc[i, o] = value
                continue
            rsend[i, o] = value.astype(BF16)
            c = to_peer(rsend.at[i, o], rrecv.at[i, me], zo_s.at[i], zo_r.at[i], d)
            c.start()
            sent.append(c)
        zo.append(sent)

    for i in range(images):
        weight = jnp.zeros((1, coef_x.shape[1]), F32)
        for b in range(per_image):
            s = i * per_image + b
            weight = weight + coef_x[s : s + 1, :]
        value = acc[i, me] + img_ref[i].astype(F32) * wide(weight)
        for d in range(1, n):
            zo[i][d - 1].wait_recv()
            value = value + rrecv[i, source(d)].astype(F32)
        out_ref[i] = value.astype(BF16)

    for group in [zi, zm, yt, yi] + zt + yo + zo:
        for c in group:
            c.wait_send()


def on_device(
    n, dp,
    image_latents, text_states, modulation, w_qkv, w_out, q_gain, k_gain,
    branch_count, branch_sign, guide_weight,
):
    images, img_len, width = image_latents.shape
    slots, txt_len, _ = text_states.shape
    per_image = slots // images
    half = (per_image + 1) // 2
    extra = per_image - half
    full = n * width
    hd = q_gain.shape[0]
    inner = w_out.shape[0]
    heads = inner // hd
    rows = half * img_len
    keys = half * (img_len + txt_len)
    mod_rows = -(-3 * images * half // 16) * 16
    coef_rows = -(-slots // 16) * 16
    vmem = pl.BlockSpec(memory_space=pltpu.VMEM)
    smem = pl.BlockSpec(memory_space=pltpu.SMEM)
    hbm = pl.BlockSpec(memory_space=pl.ANY)
    dma = pltpu.SemaphoreType.DMA
    return pl.pallas_call(
        functools.partial(kernel, n, dp, per_image),
        out_shape=jax.ShapeDtypeStruct(image_latents.shape, BF16),
        in_specs=[smem] * 3 + [vmem] * 5 + [hbm] * 2,
        out_specs=vmem,
        scratch_shapes=[
            pltpu.VMEM((3, full, inner), BF16),
            pltpu.VMEM((n, inner, width), BF16),
            pltpu.VMEM((2, n, images, img_len, width), BF16),
            pltpu.VMEM((2, images, n, img_len, width), F32),
            pltpu.VMEM((mod_rows, width), BF16),
            pltpu.VMEM((mod_rows, width), BF16),
            pltpu.VMEM((n, mod_rows, width), BF16),
            pltpu.VMEM((images, extra, txt_len, width), BF16),
            pltpu.VMEM((images, n, half * txt_len, width), BF16),
            pltpu.VMEM((coef_rows, 128), F32),
            pltpu.VMEM((coef_rows, 128), F32),
            pltpu.VMEM((images * rows, full), BF16),
            pltpu.VMEM((half * txt_len, full), BF16),
            pltpu.VMEM((images, heads, rows, hd), BF16),
            pltpu.VMEM((images, heads, keys, hd), BF16),
            pltpu.VMEM((images, heads, keys, hd), BF16),
            pltpu.VMEM((rows, inner), BF16),
            pltpu.VMEM((images, n, img_len, width), F32),
            pltpu.VMEM((images, n, img_len, width), BF16),
            pltpu.VMEM((images, n, img_len, width), BF16),
            pltpu.VMEM((images, n, img_len, width), BF16),
            pltpu.VMEM((images, n, img_len, width), BF16),
            dma((3 + n,)),
            dma((n - 1,)), dma((n - 1,)),
            dma((n - 1,)), dma((n - 1,)),
            dma((images, n - 1)), dma((images, n - 1)),
            dma((2 + images,)), dma((2 + images,)),
            dma((n,)), dma((n,)),
            dma((images, n)), dma((images, n)),
            dma((images, n - 1)), dma((images, n - 1)),
        ],
        compiler_params=pltpu.CompilerParams(
            collective_id=0, has_side_effects=True, vmem_limit_bytes=56 * 1024 * 1024
        ),
    )(
        branch_count, branch_sign, guide_weight,
        image_latents, text_states, jnp.transpose(modulation, (1, 0, 2)),
        q_gain.reshape(1, hd), k_gain.reshape(1, hd),
        jnp.transpose(w_qkv, (1, 0, 2)), w_out,
    )


def solution(mesh):
    placed = (
        P("dp", None, "mp"),
        P("dp", None, "mp"),
        P("dp", None, "mp"),
        P(None, None, "mp"),
        P("mp", None),
        P(),
        P(),
        P("dp"),
        P("dp"),
        P("dp"),
    )
    return jax.shard_map(
        functools.partial(on_device, mesh.shape["mp"], mesh.shape["dp"]),
        mesh=mesh, in_specs=placed, out_specs=P("dp", None, "mp"), check_vma=False,
    )
```

```python
import functools

import jax
import jax.numpy as jnp
from jax import lax
from jax.experimental import pallas as pl
from jax.experimental.pallas import tpu as pltpu
from jax.sharding import PartitionSpec as P

EPS = 1e-06
MESH = pl.DeviceIdType.MESH
F32 = jnp.float32
BF16 = jnp.bfloat16


def kernel(
    n, dp, per_image,
    cnt_ref, sgn_ref, gw_ref, img_ref, txt_ref, mod_ref, qg_ref, kg_ref, w_hbm, wo_hbm,
    out_ref,
    w_v, wo_v, ximg, xhat, mod_x, mod_y, mod_g, txt_y, txt_g, coef_x, coef_y,
    nimg, ntxt, q_s, k_s, v_s, att, acc, ysend, yrecv, rsend, rrecv,
    w_sem, zi_s, zi_r, zm_s, zm_r, zt_s, zt_r, yt_s, yt_r, yi_s, yi_r, yo_s, yo_r, zo_s, zo_r,
):
    me = lax.axis_index("mp")
    mine = lax.axis_index("dp")
    partner = lax.rem(mine + dp // 2, dp)
    images, img_len, width = img_ref.shape
    txt_len = txt_ref.shape[1]
    half = (per_image + 1) // 2
    extra = per_image - half
    full = n * width
    heads, hd = q_s.shape[1], q_s.shape[3]
    rows = half * img_len
    items = images * half

    weight_copies = [
        pltpu.make_async_copy(w_hbm.at[t], w_v.at[t], w_sem.at[t]) for t in range(3)
    ] + [
        pltpu.make_async_copy(
            wo_hbm.at[:, pl.ds(o * width, width)], wo_v.at[o], w_sem.at[3 + o]
        )
        for o in range(n)
    ]
    for c in weight_copies:
        c.start()

    def peer(d):
        return lax.rem(me + d, n)

    def source(d):
        return lax.rem(me - d + n, n)

    barrier = pltpu.get_barrier_semaphore()
    for d in range(1, n):
        pl.semaphore_signal(barrier, inc=1, device_id={"mp": peer(d)}, device_id_type=MESH)
    pl.semaphore_signal(barrier, inc=1, device_id={"dp": partner}, device_id_type=MESH)

    slots = images * per_image
    row_at = lax.broadcasted_iota(jnp.int32, coef_x.shape, 0)
    top = jnp.zeros(coef_x.shape, jnp.int32)
    low = jnp.ones(coef_x.shape, jnp.int32)
    for i in range(images):
        total = jnp.int32(0)
        for b in range(per_image):
            s = i * per_image + b
            live = jnp.where(b < cnt_ref[i], gw_ref[s], 0)
            total = total + live
            top = jnp.where(row_at == s, (2 * sgn_ref[s] - 1) * live, top)
        inside = (row_at >= i * per_image) & (row_at < (i + 1) * per_image)
        low = jnp.where(inside, total, low)
    coef_x[...] = top.astype(F32) / low.astype(F32)
    own_mod = [mod_ref[t].astype(F32) for t in range(3)]
    pieces = []
    for t in range(3):
        for i in range(images):
            first = i * per_image + half
            pieces.append(own_mod[t][first : first + extra])
        pieces.append(jnp.zeros((items - images * extra, width), F32))
    pieces.append(jnp.zeros((mod_x.shape[0] - 3 * items, width), F32))
    mod_x[...] = jnp.concatenate(pieces, axis=0).astype(BF16)

    pl.semaphore_wait(barrier, n)

    def to_peer(src, dst, send, recv, d):
        return pltpu.make_async_remote_copy(
            src_ref=src, dst_ref=dst, send_sem=send.at[d - 1], recv_sem=recv.at[d - 1],
            device_id={"mp": peer(d)}, device_id_type=MESH,
        )

    def to_partner(src, dst, send, recv):
        return pltpu.make_async_remote_copy(
            src_ref=src, dst_ref=dst, send_sem=send, recv_sem=recv,
            device_id={"dp": partner}, device_id_type=MESH,
        )

    def chain(ref_of, send, recv, way, s, first=None):
        chunk = lax.rem(me - s + n, n) if way == 0 else lax.rem(me + s, n)
        target = lax.rem(me + 1, n) if way == 0 else lax.rem(me + n - 1, n)
        return pltpu.make_async_remote_copy(
            src_ref=ref_of(chunk) if first is None or s > 0 else first,
            dst_ref=ref_of(chunk), send_sem=send.at[way, s], recv_sem=recv.at[way, s],
            device_id={"mp": target}, device_id_type=MESH,
        )

    def chain_start(s, *args):
        pl.when((me >= s) & (me + 1 < n))(lambda: chain(*args[:3], 0, s, *args[3:]).start())
        pl.when((me + s < n) & (me >= 1))(lambda: chain(*args[:3], 1, s, *args[3:]).start())

    def chain_sent(s, *args):
        pl.when((me >= s) & (me + 1 < n))(lambda: chain(*args[:3], 0, s, *args[3:]).wait_send())
        pl.when((me + s < n) & (me >= 1))(lambda: chain(*args[:3], 1, s, *args[3:]).wait_send())

    def arrived(way, s):
        return me >= s + 1 if way == 0 else me + s + 1 < n

    def chain_wait(s, *args):
        for way in range(2):
            pl.when(arrived(way, s))(
                lambda way=way: chain(*args[:3], way, s, *args[3:]).wait_recv()
            )

    def near(way, s):
        return lax.rem(me - s - 1 + n, n) if way == 0 else lax.rem(me + s + 1, n)

    def pass_on(way, s):
        o = near(way, s)
        return to_partner(ximg.at[0, o], ximg.at[1, o], yi_s.at[way, s], yi_r.at[way, s])

    img_chain = (lambda o: ximg.at[0, o], zi_s, zi_r, img_ref)
    mod_chain = (lambda o: mod_g.at[o], zm_s, zm_r)
    yt = [to_partner(mod_x, mod_y, yt_s.at[0], yt_r.at[0])]
    for i in range(images):
        yt.append(
            to_partner(
                txt_ref.at[pl.ds(i * per_image + half, extra)], txt_y.at[i],
                yt_s.at[1 + i], yt_r.at[1 + i],
            )
        )
    yt.append(to_partner(coef_x, coef_y, yt_s.at[1 + images], yt_r.at[1 + images]))
    yt.append(to_partner(img_ref, ximg.at[1, me], yt_s.at[2 + images], yt_r.at[2 + images]))
    chain_start(0, *img_chain)
    for c in yt:
        c.start()
    ximg[0, me] = img_ref[...]

    yt[0].wait_recv()
    got = mod_y[...].astype(F32)
    pieces = []
    for t in range(3):
        for i in range(images):
            for k in range(half):
                s = i * per_image + k
                row = own_mod[t][s : s + 1]
                if k > 0:
                    r = t * items + i * extra + extra - k
                    row = jnp.where(cnt_ref[i] > k, row, got[r : r + 1])
                pieces.append(row)
    pieces.append(jnp.zeros((mod_g.shape[1] - 3 * items, width), F32))
    mod_g[me] = jnp.concatenate(pieces, axis=0).astype(BF16)
    chain_start(0, *mod_chain)
    zt = []

    def send_text(i):
        yt[1 + i].wait_recv()
        for k in range(half):
            own = txt_ref[i * per_image + k]
            if k > 0:
                own = jnp.where(
                    cnt_ref[i] > k, own.astype(F32), txt_y[i, extra - k].astype(F32)
                ).astype(BF16)
            txt_g[i, me, pl.ds(k * txt_len, txt_len), :] = own
        zt.append(
            [
                to_peer(txt_g.at[i, me], txt_g.at[i, me], zt_s.at[i], zt_r.at[i], d)
                for d in range(1, n)
            ]
        )
        for c in zt[i]:
            c.start()

    send_text(0)
    for s in range(n - 1):
        chain_wait(s, *img_chain)
        if s + 1 < n - 1:
            chain_start(s + 1, *img_chain)
        for way in range(2):
            pl.when(arrived(way, s))(lambda way=way, s=s: pass_on(way, s).start())
        chain_wait(s, *mod_chain)
        if s + 1 < n - 1:
            chain_start(s + 1, *mod_chain)
    for i in range(1, images):
        send_text(i)

    def normalise(parts):
        mean = sum(jnp.sum(p, axis=-1, keepdims=True) for p in parts) * (1.0 / full)
        parts = [p - mean for p in parts]
        var = sum(jnp.sum(p * p, axis=-1, keepdims=True) for p in parts) * (1.0 / full)
        scale = lax.rsqrt(var + EPS)
        return [p * scale for p in parts]

    def image_hat(who):
        for i in range(images):
            parts = normalise([ximg[who, o, i].astype(F32) for o in range(n)])
            for o in range(n):
                xhat[who, i, o] = parts[o]

    image_hat(0)
    yt[2 + images].wait_recv()
    for s in range(n - 1):
        for way in range(2):
            pl.when(arrived(way, s))(lambda way=way, s=s: pass_on(way, s).wait_recv())
    image_hat(1)

    for o in range(n):
        mods = mod_g[o].astype(F32)
        for i in range(images):
            for k in range(half):
                p = i * half + k
                who = jnp.where(cnt_ref[i] > k, 0, 1)
                hat = xhat[who, i, o]
                value = hat * (1.0 + mods[items + p : items + p + 1]) + mods[p : p + 1]
                nimg[pl.ds(p * img_len, img_len), pl.ds(o * width, width)] = value.astype(BF16)

    def rms(values, gain):
        mean = jnp.mean(values * values, axis=-1, keepdims=True)
        return values * lax.rsqrt(mean + EPS) * gain

    q_gain, k_gain = qg_ref[...], kg_ref[...]
    for t in range(3):
        weight_copies[t].wait()
        made = jnp.dot(nimg[...], w_v[t], preferred_element_type=F32)
        for h in range(heads):
            part = made[:, h * hd : (h + 1) * hd]
            if t == 0:
                part = rms(part, q_gain)
            if t == 1:
                part = rms(part, k_gain)
            part = part.astype(BF16)
            for i in range(images):
                (q_s, k_s, v_s)[t][i, h, pl.ds(0, rows), :] = part[i * rows : (i + 1) * rows]

    keys = half * (img_len + txt_len)
    q_row = lax.broadcasted_iota(jnp.int32, (rows, keys), 0)
    k_col = lax.broadcasted_iota(jnp.int32, (rows, keys), 1)
    same = jnp.zeros((rows, keys), jnp.bool_)
    for k in range(half):
        in_q = (q_row >= k * img_len) & (q_row < (k + 1) * img_len)
        in_img = (k_col >= k * img_len) & (k_col < (k + 1) * img_len)
        first = rows + k * txt_len
        in_txt = (k_col >= first) & (k_col < first + txt_len)
        same = same | (in_q & (in_img | in_txt))
    bias = jnp.where(same, 0.0, -1e30)

    yt[1 + images].wait_recv()
    for c in weight_copies[3:]:
        c.wait()

    def wide(row):
        return jnp.concatenate([row] * (width // row.shape[1]), axis=1)

    order = list(range(1, n)) + [0]
    yo = []
    zo = []

    def reduce_image(i):
        sent = []
        for at, d in enumerate(order):
            o = peer(d)
            yo[i][at].wait_recv()
            value = acc[i, o] + yrecv[i, o].astype(F32)
            if d == 0:
                acc[i, o] = value
                continue
            rsend[i, o] = value.astype(BF16)
            c = to_peer(rsend.at[i, o], rrecv.at[i, me], zo_s.at[i], zo_r.at[i], d)
            c.start()
            sent.append(c)
        zo.append(sent)

    for i in range(images):
        for c in zt[i]:
            c.wait_recv()
        if i > 0:
            reduce_image(i - 1)
        parts = normalise([txt_g[i, o].astype(F32) for o in range(n)])
        for o in range(n):
            mods = mod_g[o].astype(F32)
            for k in range(half):
                p = i * half + k
                value = parts[o][k * txt_len : (k + 1) * txt_len]
                value = value * (1.0 + mods[items + p : items + p + 1]) + mods[p : p + 1]
                ntxt[pl.ds(k * txt_len, txt_len), pl.ds(o * width, width)] = value.astype(BF16)
        for t in (1, 2):
            made = jnp.dot(ntxt[...], w_v[t], preferred_element_type=F32)
            for h in range(heads):
                part = made[:, h * hd : (h + 1) * hd]
                if t == 1:
                    part = rms(part, k_gain)
                (k_s if t == 1 else v_s)[i, h, pl.ds(rows, half * txt_len), :] = part.astype(BF16)
        for h in range(heads):
            scores = lax.dot_general(
                q_s[i, h], k_s[i, h], (((1,), (1,)), ((), ())), preferred_element_type=F32
            ) * hd ** (-0.5) + bias
            powers = jnp.exp(scores - jnp.max(scores, axis=-1, keepdims=True))
            probs = powers / jnp.sum(powers, axis=-1, keepdims=True)
            att[:, pl.ds(h * hd, hd)] = jnp.dot(
                probs.astype(BF16), v_s[i, h], preferred_element_type=F32
            ).astype(BF16)
        sent = []
        for d in order:
            o = peer(d)
            part = jnp.dot(att[...], wo_v[o], preferred_element_type=F32).astype(BF16).astype(F32)
            mods = mod_g[o].astype(F32)
            own_sum = jnp.zeros((img_len, width), F32)
            far_sum = jnp.zeros((img_len, width), F32)
            for k in range(half):
                g = 2 * items + i * half + k
                term = part[k * img_len : (k + 1) * img_len] * mods[g : g + 1]
                s = i * per_image + k
                own_sum = own_sum + term * wide(coef_x[s : s + 1, :])
                if k > 0:
                    s = i * per_image + per_image - k
                    far_sum = far_sum + term * wide(coef_y[s : s + 1, :])
            acc[i, o] = own_sum
            ysend[i, o] = far_sum.astype(BF16)
            c = to_partner(ysend.at[i, o], yrecv.at[i, o], yo_s.at[i, d], yo_r.at[i, d])
            c.start()
            sent.append(c)
        yo.append(sent)

    reduce_image(images - 1)

    for i in range(images):
        weight = jnp.zeros((1, coef_x.shape[1]), F32)
        for b in range(per_image):
            s = i * per_image + b
            weight = weight + coef_x[s : s + 1, :]
        value = acc[i, me] + img_ref[i].astype(F32) * wide(weight)
        for d in range(1, n):
            zo[i][d - 1].wait_recv()
            value = value + rrecv[i, source(d)].astype(F32)
        out_ref[i] = value.astype(BF16)

    for group in [yt] + zt + yo + zo:
        for c in group:
            c.wait_send()
    for s in range(n - 1):
        chain_sent(s, *img_chain)
        chain_sent(s, *mod_chain)
        for way in range(2):
            pl.when(arrived(way, s))(lambda way=way, s=s: pass_on(way, s).wait_send())


def on_device(
    n, dp,
    image_latents, text_states, modulation, w_qkv, w_out, q_gain, k_gain,
    branch_count, branch_sign, guide_weight,
):
    images, img_len, width = image_latents.shape
    slots, txt_len, _ = text_states.shape
    per_image = slots // images
    half = (per_image + 1) // 2
    extra = per_image - half
    full = n * width
    hd = q_gain.shape[0]
    inner = w_out.shape[0]
    heads = inner // hd
    rows = half * img_len
    keys = half * (img_len + txt_len)
    mod_rows = -(-3 * images * half // 16) * 16
    coef_rows = -(-slots // 16) * 16
    vmem = pl.BlockSpec(memory_space=pltpu.VMEM)
    smem = pl.BlockSpec(memory_space=pltpu.SMEM)
    hbm = pl.BlockSpec(memory_space=pl.ANY)
    dma = pltpu.SemaphoreType.DMA
    return pl.pallas_call(
        functools.partial(kernel, n, dp, per_image),
        out_shape=jax.ShapeDtypeStruct(image_latents.shape, BF16),
        in_specs=[smem] * 3 + [vmem] * 5 + [hbm] * 2,
        out_specs=vmem,
        scratch_shapes=[
            pltpu.VMEM((3, full, inner), BF16),
            pltpu.VMEM((n, inner, width), BF16),
            pltpu.VMEM((2, n, images, img_len, width), BF16),
            pltpu.VMEM((2, images, n, img_len, width), F32),
            pltpu.VMEM((mod_rows, width), BF16),
            pltpu.VMEM((mod_rows, width), BF16),
            pltpu.VMEM((n, mod_rows, width), BF16),
            pltpu.VMEM((images, extra, txt_len, width), BF16),
            pltpu.VMEM((images, n, half * txt_len, width), BF16),
            pltpu.VMEM((coef_rows, 128), F32),
            pltpu.VMEM((coef_rows, 128), F32),
            pltpu.VMEM((images * rows, full), BF16),
            pltpu.VMEM((half * txt_len, full), BF16),
            pltpu.VMEM((images, heads, rows, hd), BF16),
            pltpu.VMEM((images, heads, keys, hd), BF16),
            pltpu.VMEM((images, heads, keys, hd), BF16),
            pltpu.VMEM((rows, inner), BF16),
            pltpu.VMEM((images, n, img_len, width), F32),
            pltpu.VMEM((images, n, img_len, width), BF16),
            pltpu.VMEM((images, n, img_len, width), BF16),
            pltpu.VMEM((images, n, img_len, width), BF16),
            pltpu.VMEM((images, n, img_len, width), BF16),
            dma((3 + n,)),
            dma((2, n - 1)), dma((2, n - 1)),
            dma((2, n - 1)), dma((2, n - 1)),
            dma((images, n - 1)), dma((images, n - 1)),
            dma((3 + images,)), dma((3 + images,)),
            dma((2, n - 1)), dma((2, n - 1)),
            dma((images, n)), dma((images, n)),
            dma((images, n - 1)), dma((images, n - 1)),
        ],
        compiler_params=pltpu.CompilerParams(
            collective_id=0, has_side_effects=True, vmem_limit_bytes=56 * 1024 * 1024
        ),
    )(
        branch_count, branch_sign, guide_weight,
        image_latents, text_states, jnp.transpose(modulation, (1, 0, 2)),
        q_gain.reshape(1, hd), k_gain.reshape(1, hd),
        jnp.transpose(w_qkv, (1, 0, 2)), w_out,
    )


def solution(mesh):
    placed = (
        P("dp", None, "mp"),
        P("dp", None, "mp"),
        P("dp", None, "mp"),
        P(None, None, "mp"),
        P("mp", None),
        P(),
        P(),
        P("dp"),
        P("dp"),
        P("dp"),
    )
    return jax.shard_map(
        functools.partial(on_device, mesh.shape["mp"], mesh.shape["dp"]),
        mesh=mesh, in_specs=placed, out_specs=P("dp", None, "mp"), check_vma=False,
    )
```

```python
import functools

import jax
import jax.numpy as jnp
from jax import lax
from jax.experimental import pallas as pl
from jax.experimental.pallas import tpu as pltpu
from jax.sharding import PartitionSpec as P

EPS = 1e-06
MESH = pl.DeviceIdType.MESH
F32 = jnp.float32
BF16 = jnp.bfloat16


def kernel(
    n, dp, per_image,
    cnt_ref, sgn_ref, gw_ref, img_ref, txt_ref, mod_ref, qg_ref, kg_ref, w_hbm, wo_hbm,
    out_ref,
    w_v, wo_v, ximg, xhat, mod_x, mod_y, mod_g, txt_y, txt_g, coef_x, coef_y,
    nimg, ntxt, q_s, k_s, v_s, att, acc, ysend, yrecv, rsend, rrecv,
    w_sem, zi_s, zi_r, zm_s, zm_r, zt_s, zt_r, yt_s, yt_r, yi_s, yi_r, yo_s, yo_r, zo_s, zo_r,
):
    me = lax.axis_index("mp")
    mine = lax.axis_index("dp")
    partner = lax.rem(mine + dp // 2, dp)
    images, img_len, width = img_ref.shape
    txt_len = txt_ref.shape[1]
    half = (per_image + 1) // 2
    extra = per_image - half
    full = n * width
    heads, hd = q_s.shape[1], q_s.shape[3]
    rows = half * img_len
    items = images * half

    weight_copies = [
        pltpu.make_async_copy(w_hbm.at[t], w_v.at[t], w_sem.at[t]) for t in range(3)
    ] + [
        pltpu.make_async_copy(
            wo_hbm.at[:, pl.ds(o * width, width)], wo_v.at[o], w_sem.at[3 + o]
        )
        for o in range(n)
    ]
    for c in weight_copies:
        c.start()

    def peer(d):
        place = me
        for bit in (1 << b for b in range(d.bit_length()) if d >> b & 1):
            place = place + bit * (1 - 2 * lax.rem(lax.div(me, bit), 2))
        return place

    barrier = pltpu.get_barrier_semaphore()
    for d in range(1, n):
        pl.semaphore_signal(barrier, inc=1, device_id={"mp": peer(d)}, device_id_type=MESH)
    pl.semaphore_signal(barrier, inc=1, device_id={"dp": partner}, device_id_type=MESH)

    slots = images * per_image
    row_at = lax.broadcasted_iota(jnp.int32, coef_x.shape, 0)
    top = jnp.zeros(coef_x.shape, jnp.int32)
    low = jnp.ones(coef_x.shape, jnp.int32)
    for i in range(images):
        total = jnp.int32(0)
        for b in range(per_image):
            s = i * per_image + b
            live = jnp.where(b < cnt_ref[i], gw_ref[s], 0)
            total = total + live
            top = jnp.where(row_at == s, (2 * sgn_ref[s] - 1) * live, top)
        inside = (row_at >= i * per_image) & (row_at < (i + 1) * per_image)
        low = jnp.where(inside, total, low)
    coef_x[...] = top.astype(F32) / low.astype(F32)
    own_mod = [mod_ref[t].astype(F32) for t in range(3)]
    pieces = []
    for t in range(3):
        for i in range(images):
            first = i * per_image + half
            pieces.append(own_mod[t][first : first + extra])
        pieces.append(jnp.zeros((items - images * extra, width), F32))
    pieces.append(jnp.zeros((mod_x.shape[0] - 3 * items, width), F32))
    mod_x[...] = jnp.concatenate(pieces, axis=0).astype(BF16)

    pl.semaphore_wait(barrier, n)

    def to_peer(src, dst, send, recv, d):
        return pltpu.make_async_remote_copy(
            src_ref=src, dst_ref=dst, send_sem=send.at[d - 1], recv_sem=recv.at[d - 1],
            device_id={"mp": peer(d)}, device_id_type=MESH,
        )

    def to_partner(src, dst, send, recv):
        return pltpu.make_async_remote_copy(
            src_ref=src, dst_ref=dst, send_sem=send, recv_sem=recv,
            device_id={"dp": partner}, device_id_type=MESH,
        )

    zi = [to_peer(img_ref, ximg.at[0, me], zi_s, zi_r, d) for d in range(1, n)]
    yt = [to_partner(mod_x, mod_y, yt_s.at[0], yt_r.at[0])]
    for i in range(images):
        yt.append(
            to_partner(
                txt_ref.at[pl.ds(i * per_image + half, extra)], txt_y.at[i],
                yt_s.at[1 + i], yt_r.at[1 + i],
            )
        )
    yt.append(to_partner(coef_x, coef_y, yt_s.at[1 + images], yt_r.at[1 + images]))
    yi = [to_partner(img_ref, ximg.at[1, me], yi_s.at[0], yi_r.at[0])]
    for c in yt:
        c.start()
    for c in zi:
        c.start()
    yi[0].start()
    ximg[0, me] = img_ref[...]

    yt[0].wait_recv()
    got = mod_y[...].astype(F32)
    pieces = []
    for t in range(3):
        for i in range(images):
            for k in range(half):
                s = i * per_image + k
                row = own_mod[t][s : s + 1]
                if k > 0:
                    r = t * items + i * extra + extra - k
                    row = jnp.where(cnt_ref[i] > k, row, got[r : r + 1])
                pieces.append(row)
    pieces.append(jnp.zeros((mod_g.shape[1] - 3 * items, width), F32))
    mod_g[me] = jnp.concatenate(pieces, axis=0).astype(BF16)
    zm = [to_peer(mod_g.at[me], mod_g.at[me], zm_s, zm_r, d) for d in range(1, n)]
    for c in zm:
        c.start()
    zt = []
    for i in range(images):
        yt[1 + i].wait_recv()
        for k in range(half):
            own = txt_ref[i * per_image + k]
            if k > 0:
                own = jnp.where(
                    cnt_ref[i] > k, own.astype(F32), txt_y[i, extra - k].astype(F32)
                ).astype(BF16)
            txt_g[i, me, pl.ds(k * txt_len, txt_len), :] = own
        zt.append(
            [
                to_peer(txt_g.at[i, me], txt_g.at[i, me], zt_s.at[i], zt_r.at[i], d)
                for d in range(1, n)
            ]
        )
        for c in reversed(zt[i]):
            c.start()

    for d in range(1, n):
        zi[d - 1].wait_recv()
        o = peer(d)
        c = to_partner(ximg.at[0, o], ximg.at[1, o], yi_s.at[d], yi_r.at[d])
        c.start()
        yi.append(c)

    def normalise(parts):
        mean = sum(jnp.sum(p, axis=-1, keepdims=True) for p in parts) * (1.0 / full)
        parts = [p - mean for p in parts]
        var = sum(jnp.sum(p * p, axis=-1, keepdims=True) for p in parts) * (1.0 / full)
        scale = lax.rsqrt(var + EPS)
        return [p * scale for p in parts]

    def image_hat(who):
        for i in range(images):
            parts = normalise([ximg[who, o, i].astype(F32) for o in range(n)])
            for o in range(n):
                xhat[who, i, o] = parts[o]

    image_hat(0)
    for c in zm:
        c.wait_recv()
    for c in yi:
        c.wait_recv()
    image_hat(1)

    for o in range(n):
        mods = mod_g[o].astype(F32)
        for i in range(images):
            for k in range(half):
                p = i * half + k
                who = jnp.where(cnt_ref[i] > k, 0, 1)
                hat = xhat[who, i, o]
                value = hat * (1.0 + mods[items + p : items + p + 1]) + mods[p : p + 1]
                nimg[pl.ds(p * img_len, img_len), pl.ds(o * width, width)] = value.astype(BF16)

    def rms(values, gain):
        mean = jnp.mean(values * values, axis=-1, keepdims=True)
        return values * lax.rsqrt(mean + EPS) * gain

    q_gain, k_gain = qg_ref[...], kg_ref[...]
    for t in range(3):
        weight_copies[t].wait()
        made = jnp.dot(nimg[...], w_v[t], preferred_element_type=F32)
        for h in range(heads):
            part = made[:, h * hd : (h + 1) * hd]
            if t == 0:
                part = rms(part, q_gain)
            if t == 1:
                part = rms(part, k_gain)
            part = part.astype(BF16)
            for i in range(images):
                (q_s, k_s, v_s)[t][i, h, pl.ds(0, rows), :] = part[i * rows : (i + 1) * rows]

    keys = half * (img_len + txt_len)
    q_row = lax.broadcasted_iota(jnp.int32, (rows, keys), 0)
    k_col = lax.broadcasted_iota(jnp.int32, (rows, keys), 1)
    same = jnp.zeros((rows, keys), jnp.bool_)
    for k in range(half):
        in_q = (q_row >= k * img_len) & (q_row < (k + 1) * img_len)
        in_img = (k_col >= k * img_len) & (k_col < (k + 1) * img_len)
        first = rows + k * txt_len
        in_txt = (k_col >= first) & (k_col < first + txt_len)
        same = same | (in_q & (in_img | in_txt))
    bias = jnp.where(same, 0.0, -1e30)

    yt[1 + images].wait_recv()
    for c in weight_copies[3:]:
        c.wait()

    def wide(row):
        return jnp.concatenate([row] * (width // row.shape[1]), axis=1)

    order = list(range(n - 1, -1, -1))
    yo = []
    zo = [[] for _ in range(images)]

    def reduce_chunk(i, at):
        d = order[at]
        o = peer(d)
        yo[i][at].wait_recv()
        value = acc[i, o] + yrecv[i, o].astype(F32)
        if d == 0:
            acc[i, o] = value
            return
        rsend[i, o] = value.astype(BF16)
        c = to_peer(rsend.at[i, o], rrecv.at[i, me], zo_s.at[i], zo_r.at[i], d)
        c.start()
        zo[i].append(c)

    for i in range(images):
        for c in zt[i]:
            c.wait_recv()
        parts = normalise([txt_g[i, o].astype(F32) for o in range(n)])
        for o in range(n):
            mods = mod_g[o].astype(F32)
            for k in range(half):
                p = i * half + k
                value = parts[o][k * txt_len : (k + 1) * txt_len]
                value = value * (1.0 + mods[items + p : items + p + 1]) + mods[p : p + 1]
                ntxt[pl.ds(k * txt_len, txt_len), pl.ds(o * width, width)] = value.astype(BF16)
        for t in (1, 2):
            made = jnp.dot(ntxt[...], w_v[t], preferred_element_type=F32)
            for h in range(heads):
                part = made[:, h * hd : (h + 1) * hd]
                if t == 1:
                    part = rms(part, k_gain)
                (k_s if t == 1 else v_s)[i, h, pl.ds(rows, half * txt_len), :] = part.astype(BF16)
        for h in range(heads):
            if i > 0:
                for at in range(h * n // heads, (h + 1) * n // heads):
                    reduce_chunk(i - 1, at)
            scores = lax.dot_general(
                q_s[i, h], k_s[i, h], (((1,), (1,)), ((), ())), preferred_element_type=F32
            ) * hd ** (-0.5) + bias
            powers = jnp.exp(scores - jnp.max(scores, axis=-1, keepdims=True))
            probs = powers / jnp.sum(powers, axis=-1, keepdims=True)
            att[:, pl.ds(h * hd, hd)] = jnp.dot(
                probs.astype(BF16), v_s[i, h], preferred_element_type=F32
            ).astype(BF16)
        sent = []
        for d in order:
            o = peer(d)
            part = jnp.dot(att[...], wo_v[o], preferred_element_type=F32).astype(BF16).astype(F32)
            mods = mod_g[o].astype(F32)
            own_sum = jnp.zeros((img_len, width), F32)
            far_sum = jnp.zeros((img_len, width), F32)
            for k in range(half):
                g = 2 * items + i * half + k
                term = part[k * img_len : (k + 1) * img_len] * mods[g : g + 1]
                s = i * per_image + k
                own_sum = own_sum + term * wide(coef_x[s : s + 1, :])
                if k > 0:
                    s = i * per_image + per_image - k
                    far_sum = far_sum + term * wide(coef_y[s : s + 1, :])
            acc[i, o] = own_sum
            ysend[i, o] = far_sum.astype(BF16)
            c = to_partner(ysend.at[i, o], yrecv.at[i, o], yo_s.at[i, d], yo_r.at[i, d])
            c.start()
            sent.append(c)
        yo.append(sent)

    for at in range(n):
        reduce_chunk(images - 1, at)

    for i in range(images):
        weight = jnp.zeros((1, coef_x.shape[1]), F32)
        for b in range(per_image):
            s = i * per_image + b
            weight = weight + coef_x[s : s + 1, :]
        value = acc[i, me] + img_ref[i].astype(F32) * wide(weight)
        for d in range(1, n):
            zo[i][order.index(d)].wait_recv()
            value = value + rrecv[i, peer(d)].astype(F32)
        out_ref[i] = value.astype(BF16)

    for group in [zi, zm, yt, yi] + zt + yo + zo:
        for c in group:
            c.wait_send()


def on_device(
    n, dp,
    image_latents, text_states, modulation, w_qkv, w_out, q_gain, k_gain,
    branch_count, branch_sign, guide_weight,
):
    images, img_len, width = image_latents.shape
    slots, txt_len, _ = text_states.shape
    per_image = slots // images
    half = (per_image + 1) // 2
    extra = per_image - half
    full = n * width
    hd = q_gain.shape[0]
    inner = w_out.shape[0]
    heads = inner // hd
    rows = half * img_len
    keys = half * (img_len + txt_len)
    mod_rows = -(-3 * images * half // 16) * 16
    coef_rows = -(-slots // 16) * 16
    vmem = pl.BlockSpec(memory_space=pltpu.VMEM)
    smem = pl.BlockSpec(memory_space=pltpu.SMEM)
    hbm = pl.BlockSpec(memory_space=pl.ANY)
    dma = pltpu.SemaphoreType.DMA
    return pl.pallas_call(
        functools.partial(kernel, n, dp, per_image),
        out_shape=jax.ShapeDtypeStruct(image_latents.shape, BF16),
        in_specs=[smem] * 3 + [vmem] * 5 + [hbm] * 2,
        out_specs=vmem,
        scratch_shapes=[
            pltpu.VMEM((3, full, inner), BF16),
            pltpu.VMEM((n, inner, width), BF16),
            pltpu.VMEM((2, n, images, img_len, width), BF16),
            pltpu.VMEM((2, images, n, img_len, width), F32),
            pltpu.VMEM((mod_rows, width), BF16),
            pltpu.VMEM((mod_rows, width), BF16),
            pltpu.VMEM((n, mod_rows, width), BF16),
            pltpu.VMEM((images, extra, txt_len, width), BF16),
            pltpu.VMEM((images, n, half * txt_len, width), BF16),
            pltpu.VMEM((coef_rows, 128), F32),
            pltpu.VMEM((coef_rows, 128), F32),
            pltpu.VMEM((images * rows, full), BF16),
            pltpu.VMEM((half * txt_len, full), BF16),
            pltpu.VMEM((images, heads, rows, hd), BF16),
            pltpu.VMEM((images, heads, keys, hd), BF16),
            pltpu.VMEM((images, heads, keys, hd), BF16),
            pltpu.VMEM((rows, inner), BF16),
            pltpu.VMEM((images, n, img_len, width), F32),
            pltpu.VMEM((images, n, img_len, width), BF16),
            pltpu.VMEM((images, n, img_len, width), BF16),
            pltpu.VMEM((images, n, img_len, width), BF16),
            pltpu.VMEM((images, n, img_len, width), BF16),
            dma((3 + n,)),
            dma((n - 1,)), dma((n - 1,)),
            dma((n - 1,)), dma((n - 1,)),
            dma((images, n - 1)), dma((images, n - 1)),
            dma((2 + images,)), dma((2 + images,)),
            dma((n,)), dma((n,)),
            dma((images, n)), dma((images, n)),
            dma((images, n - 1)), dma((images, n - 1)),
        ],
        compiler_params=pltpu.CompilerParams(
            collective_id=0, has_side_effects=True, vmem_limit_bytes=56 * 1024 * 1024
        ),
    )(
        branch_count, branch_sign, guide_weight,
        image_latents, text_states, jnp.transpose(modulation, (1, 0, 2)),
        q_gain.reshape(1, hd), k_gain.reshape(1, hd),
        jnp.transpose(w_qkv, (1, 0, 2)), w_out,
    )


def solution(mesh):
    placed = (
        P("dp", None, "mp"),
        P("dp", None, "mp"),
        P("dp", None, "mp"),
        P(None, None, "mp"),
        P("mp", None),
        P(),
        P(),
        P("dp"),
        P("dp"),
        P("dp"),
    )
    return jax.shard_map(
        functools.partial(on_device, mesh.shape["mp"], mesh.shape["dp"]),
        mesh=mesh, in_specs=placed, out_specs=P("dp", None, "mp"), check_vma=False,
    )
```

```python
import functools

import jax
import jax.numpy as jnp
from jax import lax
from jax.experimental import pallas as pl
from jax.experimental.pallas import tpu as pltpu
from jax.sharding import PartitionSpec as P

EPS = 1e-06
MESH = pl.DeviceIdType.MESH
F32 = jnp.float32
BF16 = jnp.bfloat16


def kernel(
    n, dp, per_image,
    cnt_ref, sgn_ref, gw_ref, img_ref, txt_ref, mod_ref, qg_ref, kg_ref, w_hbm, wo_hbm,
    out_ref,
    w_v, wo_v, ximg, xhat, mod_x, mod_y, mod_g, txt_y, txt_g, coef_x, coef_y,
    nimg, ntxt, q_s, k_s, v_s, att, acc, ysend, yrecv, rsend, rrecv,
    w_sem, zi_s, zi_r, zm_s, zm_r, zt_s, zt_r, yt_s, yt_r, yi_s, yi_r, yo_s, yo_r, zo_s, zo_r,
):
    me = lax.axis_index("mp")
    mine = lax.axis_index("dp")
    partner = lax.rem(mine + dp // 2, dp)
    images, img_len, width = img_ref.shape
    txt_len = txt_ref.shape[1]
    half = (per_image + 1) // 2
    extra = per_image - half
    full = n * width
    heads, hd = q_s.shape[1], q_s.shape[3]
    rows = half * img_len
    items = images * half

    weight_copies = [
        pltpu.make_async_copy(w_hbm.at[t], w_v.at[t], w_sem.at[t]) for t in range(3)
    ] + [
        pltpu.make_async_copy(
            wo_hbm.at[:, pl.ds(o * width, width)], wo_v.at[o], w_sem.at[3 + o]
        )
        for o in range(n)
    ]
    for c in weight_copies:
        c.start()

    def peer(d):
        place = me
        for bit in (1 << b for b in range(d.bit_length()) if d >> b & 1):
            place = place + bit * (1 - 2 * lax.rem(lax.div(me, bit), 2))
        return place

    barrier = pltpu.get_barrier_semaphore()
    for d in range(1, n):
        pl.semaphore_signal(barrier, inc=1, device_id={"mp": peer(d)}, device_id_type=MESH)
    pl.semaphore_signal(barrier, inc=1, device_id={"dp": partner}, device_id_type=MESH)

    slots = images * per_image
    row_at = lax.broadcasted_iota(jnp.int32, coef_x.shape, 0)
    top = jnp.zeros(coef_x.shape, jnp.int32)
    low = jnp.ones(coef_x.shape, jnp.int32)
    for i in range(images):
        total = jnp.int32(0)
        for b in range(per_image):
            s = i * per_image + b
            live = jnp.where(b < cnt_ref[i], gw_ref[s], 0)
            total = total + live
            top = jnp.where(row_at == s, (2 * sgn_ref[s] - 1) * live, top)
        inside = (row_at >= i * per_image) & (row_at < (i + 1) * per_image)
        low = jnp.where(inside, total, low)
    coef_x[...] = top.astype(F32) / low.astype(F32)
    own_mod = [mod_ref[t].astype(F32) for t in range(3)]
    pieces = []
    for t in range(3):
        for i in range(images):
            first = i * per_image + half
            pieces.append(own_mod[t][first : first + extra])
        pieces.append(jnp.zeros((items - images * extra, width), F32))
    pieces.append(jnp.zeros((mod_x.shape[0] - 3 * items, width), F32))
    mod_x[...] = jnp.concatenate(pieces, axis=0).astype(BF16)

    pl.semaphore_wait(barrier, n)

    def to_peer(src, dst, send, recv, d):
        return pltpu.make_async_remote_copy(
            src_ref=src, dst_ref=dst, send_sem=send.at[d - 1], recv_sem=recv.at[d - 1],
            device_id={"mp": peer(d)}, device_id_type=MESH,
        )

    def to_partner(src, dst, send, recv):
        return pltpu.make_async_remote_copy(
            src_ref=src, dst_ref=dst, send_sem=send, recv_sem=recv,
            device_id={"dp": partner}, device_id_type=MESH,
        )

    zi = [to_peer(img_ref, ximg.at[0, me], zi_s, zi_r, d) for d in range(1, n)]
    yt = [to_partner(mod_x, mod_y, yt_s.at[0], yt_r.at[0])]
    for i in range(images):
        yt.append(
            to_partner(
                txt_ref.at[pl.ds(i * per_image + half, extra)], txt_y.at[i],
                yt_s.at[1 + i], yt_r.at[1 + i],
            )
        )
    yt.append(to_partner(coef_x, coef_y, yt_s.at[1 + images], yt_r.at[1 + images]))
    yi = [to_partner(img_ref, ximg.at[1, me], yi_s.at[0], yi_r.at[0])]
    for c in yt:
        c.start()
    for c in zi:
        c.start()
    yi[0].start()
    ximg[0, me] = img_ref[...]

    yt[0].wait_recv()
    got = mod_y[...].astype(F32)
    pieces = []
    for t in range(3):
        for i in range(images):
            for k in range(half):
                s = i * per_image + k
                row = own_mod[t][s : s + 1]
                if k > 0:
                    r = t * items + i * extra + extra - k
                    row = jnp.where(cnt_ref[i] > k, row, got[r : r + 1])
                pieces.append(row)
    pieces.append(jnp.zeros((mod_g.shape[1] - 3 * items, width), F32))
    mod_g[me] = jnp.concatenate(pieces, axis=0).astype(BF16)
    zm = [to_peer(mod_g.at[me], mod_g.at[me], zm_s, zm_r, d) for d in range(1, n)]
    for c in zm:
        c.start()
    zt = []
    for i in range(images):
        yt[1 + i].wait_recv()
        for k in range(half):
            own = txt_ref[i * per_image + k]
            if k > 0:
                own = jnp.where(
                    cnt_ref[i] > k, own.astype(F32), txt_y[i, extra - k].astype(F32)
                ).astype(BF16)
            txt_g[i, me, pl.ds(k * txt_len, txt_len), :] = own
        zt.append(
            [
                to_peer(txt_g.at[i, me], txt_g.at[i, me], zt_s.at[i], zt_r.at[i], d)
                for d in range(1, n)
            ]
        )
        for c in reversed(zt[i]):
            c.start()

    for d in range(1, n):
        zi[d - 1].wait_recv()
        o = peer(d)
        c = to_partner(ximg.at[0, o], ximg.at[1, o], yi_s.at[d], yi_r.at[d])
        c.start()
        yi.append(c)

    def normalise(parts):
        mean = sum(jnp.sum(p, axis=-1, keepdims=True) for p in parts) * (1.0 / full)
        parts = [p - mean for p in parts]
        var = sum(jnp.sum(p * p, axis=-1, keepdims=True) for p in parts) * (1.0 / full)
        scale = lax.rsqrt(var + EPS)
        return [p * scale for p in parts]

    def image_hat(who):
        for i in range(images):
            parts = normalise([ximg[who, o, i].astype(F32) for o in range(n)])
            for o in range(n):
                xhat[who, i, o] = parts[o]

    image_hat(0)
    for c in zm:
        c.wait_recv()
    for c in yi:
        c.wait_recv()
    image_hat(1)

    for o in range(n):
        mods = mod_g[o].astype(F32)
        for i in range(images):
            for k in range(half):
                p = i * half + k
                who = jnp.where(cnt_ref[i] > k, 0, 1)
                hat = xhat[who, i, o]
                value = hat * (1.0 + mods[items + p : items + p + 1]) + mods[p : p + 1]
                nimg[pl.ds(p * img_len, img_len), pl.ds(o * width, width)] = value.astype(BF16)

    def rms(values, gain):
        mean = jnp.mean(values * values, axis=-1, keepdims=True)
        return values * lax.rsqrt(mean + EPS) * gain

    q_gain, k_gain = qg_ref[...], kg_ref[...]
    for t in range(3):
        weight_copies[t].wait()
        made = jnp.dot(nimg[...], w_v[t], preferred_element_type=F32)
        for h in range(heads):
            part = made[:, h * hd : (h + 1) * hd]
            if t == 0:
                part = rms(part, q_gain)
            if t == 1:
                part = rms(part, k_gain)
            part = part.astype(BF16)
            for i in range(images):
                (q_s, k_s, v_s)[t][i, h, pl.ds(0, rows), :] = part[i * rows : (i + 1) * rows]

    keys = half * (img_len + txt_len)
    q_row = lax.broadcasted_iota(jnp.int32, (rows, keys), 0)
    k_col = lax.broadcasted_iota(jnp.int32, (rows, keys), 1)
    same = jnp.zeros((rows, keys), jnp.bool_)
    for k in range(half):
        in_q = (q_row >= k * img_len) & (q_row < (k + 1) * img_len)
        in_img = (k_col >= k * img_len) & (k_col < (k + 1) * img_len)
        first = rows + k * txt_len
        in_txt = (k_col >= first) & (k_col < first + txt_len)
        same = same | (in_q & (in_img | in_txt))
    bias = jnp.where(same, 0.0, -1e30)

    yt[1 + images].wait_recv()
    for c in weight_copies[3:]:
        c.wait()

    def wide(row):
        return jnp.concatenate([row] * (width // row.shape[1]), axis=1)

    order = list(range(n - 1, -1, -1))
    yo = []
    zo = [[] for _ in range(images)]

    def reduce_chunk(i, at):
        d = order[at]
        o = peer(d)
        yo[i][at].wait_recv()
        value = acc[i, o] + yrecv[i, o].astype(F32)
        if d == 0:
            acc[i, o] = value
            return
        rsend[i, o] = value.astype(BF16)
        c = to_peer(rsend.at[i, o], rrecv.at[i, me], zo_s.at[i], zo_r.at[i], d)
        c.start()
        zo[i].append(c)

    for i in range(images):
        for c in zt[i]:
            c.wait_recv()
        parts = normalise([txt_g[i, o].astype(F32) for o in range(n)])
        for o in range(n):
            mods = mod_g[o].astype(F32)
            for k in range(half):
                p = i * half + k
                value = parts[o][k * txt_len : (k + 1) * txt_len]
                value = value * (1.0 + mods[items + p : items + p + 1]) + mods[p : p + 1]
                ntxt[pl.ds(p * txt_len, txt_len), pl.ds(o * width, width)] = value.astype(BF16)
    tail = half * txt_len
    for t in (1, 2):
        made = jnp.dot(ntxt[...], w_v[t], preferred_element_type=F32)
        for h in range(heads):
            part = made[:, h * hd : (h + 1) * hd]
            if t == 1:
                part = rms(part, k_gain)
            part = part.astype(BF16)
            for i in range(images):
                (k_s if t == 1 else v_s)[i, h, pl.ds(rows, tail), :] = part[
                    i * tail : (i + 1) * tail
                ]

    for i in range(images):
        for h in range(heads):
            scores = lax.dot_general(
                q_s[i, h], k_s[i, h], (((1,), (1,)), ((), ())), preferred_element_type=F32
            ) * hd ** (-0.5) + bias
            powers = jnp.exp(scores - jnp.max(scores, axis=-1, keepdims=True))
            probs = powers / jnp.sum(powers, axis=-1, keepdims=True)
            att[:, pl.ds(h * hd, hd)] = jnp.dot(
                probs.astype(BF16), v_s[i, h], preferred_element_type=F32
            ).astype(BF16)
        sent = []
        for at, d in enumerate(order):
            o = peer(d)
            part = jnp.dot(att[...], wo_v[o], preferred_element_type=F32).astype(BF16).astype(F32)
            mods = mod_g[o].astype(F32)
            own_sum = jnp.zeros((img_len, width), F32)
            far_sum = jnp.zeros((img_len, width), F32)
            for k in range(half):
                g = 2 * items + i * half + k
                term = part[k * img_len : (k + 1) * img_len] * mods[g : g + 1]
                s = i * per_image + k
                own_sum = own_sum + term * wide(coef_x[s : s + 1, :])
                if k > 0:
                    s = i * per_image + per_image - k
                    far_sum = far_sum + term * wide(coef_y[s : s + 1, :])
            acc[i, o] = own_sum
            ysend[i, o] = far_sum.astype(BF16)
            c = to_partner(ysend.at[i, o], yrecv.at[i, o], yo_s.at[i, d], yo_r.at[i, d])
            c.start()
            sent.append(c)
            if i > 0:
                reduce_chunk(i - 1, at)
        yo.append(sent)

    for at in range(n):
        reduce_chunk(images - 1, at)

    for i in range(images):
        weight = jnp.zeros((1, coef_x.shape[1]), F32)
        for b in range(per_image):
            s = i * per_image + b
            weight = weight + coef_x[s : s + 1, :]
        value = acc[i, me] + img_ref[i].astype(F32) * wide(weight)
        for d in range(1, n):
            zo[i][order.index(d)].wait_recv()
            value = value + rrecv[i, peer(d)].astype(F32)
        out_ref[i] = value.astype(BF16)

    for group in [zi, zm, yt, yi] + zt + yo + zo:
        for c in group:
            c.wait_send()


def on_device(
    n, dp,
    image_latents, text_states, modulation, w_qkv, w_out, q_gain, k_gain,
    branch_count, branch_sign, guide_weight,
):
    images, img_len, width = image_latents.shape
    slots, txt_len, _ = text_states.shape
    per_image = slots // images
    half = (per_image + 1) // 2
    extra = per_image - half
    full = n * width
    hd = q_gain.shape[0]
    inner = w_out.shape[0]
    heads = inner // hd
    rows = half * img_len
    keys = half * (img_len + txt_len)
    mod_rows = -(-3 * images * half // 16) * 16
    coef_rows = -(-slots // 16) * 16
    vmem = pl.BlockSpec(memory_space=pltpu.VMEM)
    smem = pl.BlockSpec(memory_space=pltpu.SMEM)
    hbm = pl.BlockSpec(memory_space=pl.ANY)
    dma = pltpu.SemaphoreType.DMA
    return pl.pallas_call(
        functools.partial(kernel, n, dp, per_image),
        out_shape=jax.ShapeDtypeStruct(image_latents.shape, BF16),
        in_specs=[smem] * 3 + [vmem] * 5 + [hbm] * 2,
        out_specs=vmem,
        scratch_shapes=[
            pltpu.VMEM((3, full, inner), BF16),
            pltpu.VMEM((n, inner, width), BF16),
            pltpu.VMEM((2, n, images, img_len, width), BF16),
            pltpu.VMEM((2, images, n, img_len, width), F32),
            pltpu.VMEM((mod_rows, width), BF16),
            pltpu.VMEM((mod_rows, width), BF16),
            pltpu.VMEM((n, mod_rows, width), BF16),
            pltpu.VMEM((images, extra, txt_len, width), BF16),
            pltpu.VMEM((images, n, half * txt_len, width), BF16),
            pltpu.VMEM((coef_rows, 128), F32),
            pltpu.VMEM((coef_rows, 128), F32),
            pltpu.VMEM((images * rows, full), BF16),
            pltpu.VMEM((images * half * txt_len, full), BF16),
            pltpu.VMEM((images, heads, rows, hd), BF16),
            pltpu.VMEM((images, heads, keys, hd), BF16),
            pltpu.VMEM((images, heads, keys, hd), BF16),
            pltpu.VMEM((rows, inner), BF16),
            pltpu.VMEM((images, n, img_len, width), F32),
            pltpu.VMEM((images, n, img_len, width), BF16),
            pltpu.VMEM((images, n, img_len, width), BF16),
            pltpu.VMEM((images, n, img_len, width), BF16),
            pltpu.VMEM((images, n, img_len, width), BF16),
            dma((3 + n,)),
            dma((n - 1,)), dma((n - 1,)),
            dma((n - 1,)), dma((n - 1,)),
            dma((images, n - 1)), dma((images, n - 1)),
            dma((2 + images,)), dma((2 + images,)),
            dma((n,)), dma((n,)),
            dma((images, n)), dma((images, n)),
            dma((images, n - 1)), dma((images, n - 1)),
        ],
        compiler_params=pltpu.CompilerParams(
            collective_id=0, has_side_effects=True, vmem_limit_bytes=56 * 1024 * 1024
        ),
    )(
        branch_count, branch_sign, guide_weight,
        image_latents, text_states, jnp.transpose(modulation, (1, 0, 2)),
        q_gain.reshape(1, hd), k_gain.reshape(1, hd),
        jnp.transpose(w_qkv, (1, 0, 2)), w_out,
    )


def solution(mesh):
    placed = (
        P("dp", None, "mp"),
        P("dp", None, "mp"),
        P("dp", None, "mp"),
        P(None, None, "mp"),
        P("mp", None),
        P(),
        P(),
        P("dp"),
        P("dp"),
        P("dp"),
    )
    return jax.shard_map(
        functools.partial(on_device, mesh.shape["mp"], mesh.shape["dp"]),
        mesh=mesh, in_specs=placed, out_specs=P("dp", None, "mp"), check_vma=False,
    )
```

```python
import functools

import jax
import jax.numpy as jnp
from jax import lax
from jax.experimental import pallas as pl
from jax.experimental.pallas import tpu as pltpu
from jax.sharding import PartitionSpec as P

EPS = 1e-06
MESH = pl.DeviceIdType.MESH
F32 = jnp.float32
BF16 = jnp.bfloat16


def kernel(
    n, dp, per_image,
    cnt_ref, sgn_ref, gw_ref, img_ref, txt_ref, mod_ref, qg_ref, kg_ref, w_hbm, wo_hbm,
    out_ref,
    w_v, wo_v, ximg, xhat, mod_x, mod_y, mod_g, txt_y, txt_g, coef_x, coef_y,
    nimg, ntxt, q_s, k_s, v_s, att, acc, ysend, yrecv, rsend, rrecv,
    w_sem, zi_s, zi_r, zm_s, zm_r, zt_s, zt_r, yt_s, yt_r, yi_s, yi_r, yo_s, yo_r, zo_s, zo_r,
):
    me = lax.axis_index("mp")
    mine = lax.axis_index("dp")
    partner = lax.rem(mine + dp // 2, dp)
    images, img_len, width = img_ref.shape
    txt_len = txt_ref.shape[1]
    half = (per_image + 1) // 2
    extra = per_image - half
    full = n * width
    heads, hd = q_s.shape[1], q_s.shape[3]
    rows = half * img_len
    items = images * half

    weight_copies = [
        pltpu.make_async_copy(w_hbm.at[t], w_v.at[t], w_sem.at[t]) for t in range(3)
    ] + [
        pltpu.make_async_copy(
            wo_hbm.at[:, pl.ds(o * width, width)], wo_v.at[o], w_sem.at[3 + o]
        )
        for o in range(n)
    ]
    for c in weight_copies:
        c.start()

    def peer(d):
        return lax.rem(me + d, n)

    def source(d):
        return lax.rem(me - d + n, n)

    barrier = pltpu.get_barrier_semaphore()
    for d in range(1, n):
        pl.semaphore_signal(barrier, inc=1, device_id={"mp": peer(d)}, device_id_type=MESH)
    pl.semaphore_signal(barrier, inc=1, device_id={"dp": partner}, device_id_type=MESH)

    slots = images * per_image
    row_at = lax.broadcasted_iota(jnp.int32, coef_x.shape, 0)
    top = jnp.zeros(coef_x.shape, jnp.int32)
    low = jnp.ones(coef_x.shape, jnp.int32)
    for i in range(images):
        total = jnp.int32(0)
        for b in range(per_image):
            s = i * per_image + b
            live = jnp.where(b < cnt_ref[i], gw_ref[s], 0)
            total = total + live
            top = jnp.where(row_at == s, (2 * sgn_ref[s] - 1) * live, top)
        inside = (row_at >= i * per_image) & (row_at < (i + 1) * per_image)
        low = jnp.where(inside, total, low)
    coef_x[...] = top.astype(F32) / low.astype(F32)
    own_mod = [mod_ref[t].astype(F32) for t in range(3)]
    pieces = []
    for t in range(3):
        for i in range(images):
            first = i * per_image + half
            pieces.append(own_mod[t][first : first + extra])
        pieces.append(jnp.zeros((items - images * extra, width), F32))
    pieces.append(jnp.zeros((mod_x.shape[0] - 3 * items, width), F32))
    mod_x[...] = jnp.concatenate(pieces, axis=0).astype(BF16)

    pl.semaphore_wait(barrier, n)

    def to_peer(src, dst, send, recv, d):
        return pltpu.make_async_remote_copy(
            src_ref=src, dst_ref=dst, send_sem=send.at[d - 1], recv_sem=recv.at[d - 1],
            device_id={"mp": peer(d)}, device_id_type=MESH,
        )

    def to_partner(src, dst, send, recv):
        return pltpu.make_async_remote_copy(
            src_ref=src, dst_ref=dst, send_sem=send, recv_sem=recv,
            device_id={"dp": partner}, device_id_type=MESH,
        )

    zi = [to_peer(img_ref, ximg.at[0, me], zi_s, zi_r, d) for d in range(1, n)]
    yt = [to_partner(mod_x, mod_y, yt_s.at[0], yt_r.at[0])]
    for i in range(images):
        yt.append(
            to_partner(
                txt_ref.at[pl.ds(i * per_image + half, extra)], txt_y.at[i],
                yt_s.at[1 + i], yt_r.at[1 + i],
            )
        )
    yt.append(to_partner(coef_x, coef_y, yt_s.at[1 + images], yt_r.at[1 + images]))
    yi = [to_partner(img_ref, ximg.at[1, me], yi_s.at[0], yi_r.at[0])]
    for c in yt:
        c.start()
    for c in zi:
        c.start()
    yi[0].start()
    ximg[0, me] = img_ref[...]

    yt[0].wait_recv()
    got = mod_y[...].astype(F32)
    pieces = []
    for t in range(3):
        for i in range(images):
            for k in range(half):
                s = i * per_image + k
                row = own_mod[t][s : s + 1]
                if k > 0:
                    r = t * items + i * extra + extra - k
                    row = jnp.where(cnt_ref[i] > k, row, got[r : r + 1])
                pieces.append(row)
    pieces.append(jnp.zeros((mod_g.shape[1] - 3 * items, width), F32))
    mod_g[me] = jnp.concatenate(pieces, axis=0).astype(BF16)
    zm = [to_peer(mod_g.at[me], mod_g.at[me], zm_s, zm_r, d) for d in range(1, n)]
    for c in zm:
        c.start()
    zt = []
    for i in range(images):
        yt[1 + i].wait_recv()
        for k in range(half):
            own = txt_ref[i * per_image + k]
            if k > 0:
                own = jnp.where(
                    cnt_ref[i] > k, own.astype(F32), txt_y[i, extra - k].astype(F32)
                ).astype(BF16)
            txt_g[i, me, pl.ds(k * txt_len, txt_len), :] = own
        zt.append(
            [
                to_peer(txt_g.at[i, me], txt_g.at[i, me], zt_s.at[i], zt_r.at[i], d)
                for d in range(1, n)
            ]
        )
        for c in zt[i]:
            c.start()

    for d in range(1, n):
        zi[d - 1].wait_recv()
        o = source(d)
        c = to_partner(ximg.at[0, o], ximg.at[1, o], yi_s.at[d], yi_r.at[d])
        c.start()
        yi.append(c)

    def normalise(parts):
        mean = sum(jnp.sum(p, axis=-1, keepdims=True) for p in parts) * (1.0 / full)
        parts = [p - mean for p in parts]
        var = sum(jnp.sum(p * p, axis=-1, keepdims=True) for p in parts) * (1.0 / full)
        scale = lax.rsqrt(var + EPS)
        return [p * scale for p in parts]

    def image_hat(who):
        for i in range(images):
            parts = normalise([ximg[who, o, i].astype(F32) for o in range(n)])
            for o in range(n):
                xhat[who, i, o] = parts[o]

    image_hat(0)
    for c in zm:
        c.wait_recv()
    for c in yi:
        c.wait_recv()
    image_hat(1)

    for o in range(n):
        mods = mod_g[o].astype(F32)
        for i in range(images):
            for k in range(half):
                p = i * half + k
                who = jnp.where(cnt_ref[i] > k, 0, 1)
                hat = xhat[who, i, o]
                value = hat * (1.0 + mods[items + p : items + p + 1]) + mods[p : p + 1]
                nimg[pl.ds(p * img_len, img_len), pl.ds(o * width, width)] = value.astype(BF16)

    def rms(values, gain):
        mean = jnp.mean(values * values, axis=-1, keepdims=True)
        return values * lax.rsqrt(mean + EPS) * gain

    q_gain, k_gain = qg_ref[...], kg_ref[...]
    for t in range(3):
        weight_copies[t].wait()
        made = jnp.dot(nimg[...], w_v[t], preferred_element_type=F32)
        for h in range(heads):
            part = made[:, h * hd : (h + 1) * hd]
            if t == 0:
                part = rms(part, q_gain)
            if t == 1:
                part = rms(part, k_gain)
            part = part.astype(BF16)
            for i in range(images):
                (q_s, k_s, v_s)[t][i, h, pl.ds(0, rows), :] = part[i * rows : (i + 1) * rows]

    keys = half * (img_len + txt_len)
    q_row = lax.broadcasted_iota(jnp.int32, (rows, keys), 0)
    k_col = lax.broadcasted_iota(jnp.int32, (rows, keys), 1)
    same = jnp.zeros((rows, keys), jnp.bool_)
    for k in range(half):
        in_q = (q_row >= k * img_len) & (q_row < (k + 1) * img_len)
        in_img = (k_col >= k * img_len) & (k_col < (k + 1) * img_len)
        first = rows + k * txt_len
        in_txt = (k_col >= first) & (k_col < first + txt_len)
        same = same | (in_q & (in_img | in_txt))
    bias = jnp.where(same, 0.0, -1e30)

    yt[1 + images].wait_recv()
    for c in weight_copies[3:]:
        c.wait()

    def wide(row):
        return jnp.concatenate([row] * (width // row.shape[1]), axis=1)

    order = list(range(1, n)) + [0]
    yo = []
    zo = [[] for _ in range(images)]

    def reduce_chunk(i, at):
        d = order[at]
        o = peer(d)
        yo[i][at].wait_recv()
        value = acc[i, o] + yrecv[i, o].astype(F32)
        if d == 0:
            acc[i, o] = value
            return
        rsend[i, o] = value.astype(BF16)
        c = to_peer(rsend.at[i, o], rrecv.at[i, me], zo_s.at[i], zo_r.at[i], d)
        c.start()
        zo[i].append(c)

    for i in range(images):
        for c in zt[i]:
            c.wait_recv()
        parts = normalise([txt_g[i, o].astype(F32) for o in range(n)])
        for o in range(n):
            mods = mod_g[o].astype(F32)
            for k in range(half):
                p = i * half + k
                value = parts[o][k * txt_len : (k + 1) * txt_len]
                value = value * (1.0 + mods[items + p : items + p + 1]) + mods[p : p + 1]
                ntxt[pl.ds(p * txt_len, txt_len), pl.ds(o * width, width)] = value.astype(BF16)
    tail = half * txt_len
    for t in (1, 2):
        made = jnp.dot(ntxt[...], w_v[t], preferred_element_type=F32)
        for h in range(heads):
            part = made[:, h * hd : (h + 1) * hd]
            if t == 1:
                part = rms(part, k_gain)
            part = part.astype(BF16)
            for i in range(images):
                (k_s if t == 1 else v_s)[i, h, pl.ds(rows, tail), :] = part[
                    i * tail : (i + 1) * tail
                ]

    for i in range(images):
        for h in range(heads):
            scores = lax.dot_general(
                q_s[i, h], k_s[i, h], (((1,), (1,)), ((), ())), preferred_element_type=F32
            ) * hd ** (-0.5) + bias
            powers = jnp.exp(scores - jnp.max(scores, axis=-1, keepdims=True))
            probs = powers / jnp.sum(powers, axis=-1, keepdims=True)
            att[:, pl.ds(h * hd, hd)] = jnp.dot(
                probs.astype(BF16), v_s[i, h], preferred_element_type=F32
            ).astype(BF16)
        sent = []
        for at, d in enumerate(order):
            o = peer(d)
            part = jnp.dot(att[...], wo_v[o], preferred_element_type=F32).astype(BF16).astype(F32)
            mods = mod_g[o].astype(F32)
            own_sum = jnp.zeros((img_len, width), F32)
            far_sum = jnp.zeros((img_len, width), F32)
            for k in range(half):
                g = 2 * items + i * half + k
                term = part[k * img_len : (k + 1) * img_len] * mods[g : g + 1]
                s = i * per_image + k
                own_sum = own_sum + term * wide(coef_x[s : s + 1, :])
                if k > 0:
                    s = i * per_image + per_image - k
                    far_sum = far_sum + term * wide(coef_y[s : s + 1, :])
            acc[i, o] = own_sum
            ysend[i, o] = far_sum.astype(BF16)
            c = to_partner(ysend.at[i, o], yrecv.at[i, o], yo_s.at[i, d], yo_r.at[i, d])
            c.start()
            sent.append(c)
            if i > 0:
                reduce_chunk(i - 1, at)
        yo.append(sent)

    for at in range(n):
        reduce_chunk(images - 1, at)

    for i in range(images):
        weight = jnp.zeros((1, coef_x.shape[1]), F32)
        for b in range(per_image):
            s = i * per_image + b
            weight = weight + coef_x[s : s + 1, :]
        value = acc[i, me] + img_ref[i].astype(F32) * wide(weight)
        for d in range(1, n):
            zo[i][order.index(d)].wait_recv()
            value = value + rrecv[i, source(d)].astype(F32)
        out_ref[i] = value.astype(BF16)

    for group in [zi, zm, yt, yi] + zt + yo + zo:
        for c in group:
            c.wait_send()


def on_device(
    n, dp,
    image_latents, text_states, modulation, w_qkv, w_out, q_gain, k_gain,
    branch_count, branch_sign, guide_weight,
):
    images, img_len, width = image_latents.shape
    slots, txt_len, _ = text_states.shape
    per_image = slots // images
    half = (per_image + 1) // 2
    extra = per_image - half
    full = n * width
    hd = q_gain.shape[0]
    inner = w_out.shape[0]
    heads = inner // hd
    rows = half * img_len
    keys = half * (img_len + txt_len)
    mod_rows = -(-3 * images * half // 16) * 16
    coef_rows = -(-slots // 16) * 16
    vmem = pl.BlockSpec(memory_space=pltpu.VMEM)
    smem = pl.BlockSpec(memory_space=pltpu.SMEM)
    hbm = pl.BlockSpec(memory_space=pl.ANY)
    dma = pltpu.SemaphoreType.DMA
    return pl.pallas_call(
        functools.partial(kernel, n, dp, per_image),
        out_shape=jax.ShapeDtypeStruct(image_latents.shape, BF16),
        in_specs=[smem] * 3 + [vmem] * 5 + [hbm] * 2,
        out_specs=vmem,
        scratch_shapes=[
            pltpu.VMEM((3, full, inner), BF16),
            pltpu.VMEM((n, inner, width), BF16),
            pltpu.VMEM((2, n, images, img_len, width), BF16),
            pltpu.VMEM((2, images, n, img_len, width), F32),
            pltpu.VMEM((mod_rows, width), BF16),
            pltpu.VMEM((mod_rows, width), BF16),
            pltpu.VMEM((n, mod_rows, width), BF16),
            pltpu.VMEM((images, extra, txt_len, width), BF16),
            pltpu.VMEM((images, n, half * txt_len, width), BF16),
            pltpu.VMEM((coef_rows, 128), F32),
            pltpu.VMEM((coef_rows, 128), F32),
            pltpu.VMEM((images * rows, full), BF16),
            pltpu.VMEM((images * half * txt_len, full), BF16),
            pltpu.VMEM((images, heads, rows, hd), BF16),
            pltpu.VMEM((images, heads, keys, hd), BF16),
            pltpu.VMEM((images, heads, keys, hd), BF16),
            pltpu.VMEM((rows, inner), BF16),
            pltpu.VMEM((images, n, img_len, width), F32),
            pltpu.VMEM((images, n, img_len, width), BF16),
            pltpu.VMEM((images, n, img_len, width), BF16),
            pltpu.VMEM((images, n, img_len, width), BF16),
            pltpu.VMEM((images, n, img_len, width), BF16),
            dma((3 + n,)),
            dma((n - 1,)), dma((n - 1,)),
            dma((n - 1,)), dma((n - 1,)),
            dma((images, n - 1)), dma((images, n - 1)),
            dma((2 + images,)), dma((2 + images,)),
            dma((n,)), dma((n,)),
            dma((images, n)), dma((images, n)),
            dma((images, n - 1)), dma((images, n - 1)),
        ],
        compiler_params=pltpu.CompilerParams(
            collective_id=0, has_side_effects=True, vmem_limit_bytes=56 * 1024 * 1024
        ),
    )(
        branch_count, branch_sign, guide_weight,
        image_latents, text_states, jnp.transpose(modulation, (1, 0, 2)),
        q_gain.reshape(1, hd), k_gain.reshape(1, hd),
        jnp.transpose(w_qkv, (1, 0, 2)), w_out,
    )


def solution(mesh):
    placed = (
        P("dp", None, "mp"),
        P("dp", None, "mp"),
        P("dp", None, "mp"),
        P(None, None, "mp"),
        P("mp", None),
        P(),
        P(),
        P("dp"),
        P("dp"),
        P("dp"),
    )
    return jax.shard_map(
        functools.partial(on_device, mesh.shape["mp"], mesh.shape["dp"]),
        mesh=mesh, in_specs=placed, out_specs=P("dp", None, "mp"), check_vma=False,
    )
```
